1024 devices in a mesh: pipe: 8 (over z), seq: 32 (over y_hi, x), dp: 4 (over y_lo, core).
Axes of the slice: x: 8, y: 8 (y_hi: 4, y_lo: 2; y = y_hi * 2 + y_lo), z: 8, core: 2. Of those that a mesh axis runs over, the one named last changes fastest.
Arguments:
- inputs_saved: bfloat16 [8, 4, 2, 2048, 7168], P('pipe', 'dp', None, None, 'seq'), may hold values from -6 to 6
- grad_latent: bfloat16 [8, 4, 2, 2048, 384], P('pipe', 'dp', None, 'seq'), may hold values from -6 to 6
- weights: bfloat16 [8, 7168, 384], P('pipe', 'seq'), may hold values from -0.0625 to 0.0625
Outputs:
- input_grads: bfloat16 [8, 4, 2048, 7168], P('pipe', 'dp', None, 'seq')
- weight_grads: float32 [8, 7168, 384], P('pipe', 'seq', 'dp')
The draws below stay inside these ranges and needn't reach their ends.
All inputs are finite; a program needn't handle non-finite values.
Results may differ from the reference program's by a relative error of at most 0.0039.
Values may be sent and summed in bfloat16 or wider, within the bound.
No kernel may reach another device: no remote copies, remote signals or barrier semaphores. Data moves between devices by JAX's collectives and lax.ppermute only.
A program may use at most 32 MiB of HBM per device.

```python
import jax
import jax.numpy as jnp
from jax import lax

D = 7168
LAT = 384
TOKENS = 2048
N_PIPE = 8
N_DP = 4


def level_of(stream_key, shape, pieces, least, high):
    def one(axis_at, parts):
        draws = jax.random.uniform(jax.random.fold_in(jax.random.fold_in(stream_key, 6), axis_at), (parts,), jnp.float32, least / len(pieces), high / len(pieces))
        return jnp.repeat(jnp.exp(draws), shape[axis_at] // parts).reshape((-1,) + (1,) * (len(shape) - axis_at - 1))

    gain = one(*pieces[0])
    for cut in pieces[1:]:
        gain = gain * one(*cut)
    return gain


def normal_values(stream_key, shape, spread, bound, cuts=(), held_as=jnp.bfloat16):
    array = jax.random.normal(stream_key, shape, jnp.float32) * spread
    if len(cuts) > 0:
        array = level_of(stream_key, shape, cuts, -0.22, 0.18) * array
    return jnp.clip(array, min=-bound, max=bound).astype(held_as)


def setup_inputs(seed: int = 0) -> dict:
    key_of = jax.random.split(jax.random.key(seed), 4)
    inputs_saved = normal_values(key_of[0], (N_PIPE, N_DP, 2, TOKENS, D), 1.0, 6.0, ((0, 8), (1, 4), (4, 32)))
    grad_latent = normal_values(key_of[1], (N_PIPE, N_DP, 2, TOKENS, LAT), 1.0, 6.0, ((0, 8), (1, 4), (3, 32)))
    weights = normal_values(key_of[2], (N_PIPE, D, LAT), D ** -0.5, 0.0625, ((0, 8), (1, 32)))
    return dict(inputs_saved=inputs_saved, grad_latent=grad_latent, weights=weights)


def reference(inputs_saved, grad_latent, weights):
    def input_part(pair):
        grads, weight_matrix = pair
        return lax.map(lambda member: jnp.dot(member[0], weight_matrix.T, preferred_element_type=jnp.float32).astype(jnp.bfloat16), grads)

    input_grads = lax.map(input_part, (grad_latent, weights))

    def partials(pair):
        saved, grads = pair

        def one_replica(inner):
            saved_one, grads_one = inner
            first = jnp.dot(saved_one[0].T, grads_one[0], preferred_element_type=jnp.float32)
            second = jnp.dot(saved_one[1].T, grads_one[1], preferred_element_type=jnp.float32)
            return first, second

        first_all, second_all = lax.map(one_replica, (saved, grads))
        return jnp.sum(first_all, 0), jnp.sum(second_all, 0)

    grad_fwd, grad_rev = lax.map(partials, (inputs_saved, grad_latent))
    weight_grads = (grad_fwd + grad_rev[::-1]) * (1.0 / TOKENS)
    return input_grads, weight_grads
```

```python
import jax
import jax.numpy as jnp
from jax import lax
from jax.sharding import PartitionSpec as P

X_CHIPS = 8


def local(inputs_saved, grad_latent, weights):
    seq = lax.axis_size("seq")
    pipe = lax.axis_size("pipe")
    dp = lax.axis_size("dp")
    nx = X_CHIPS
    ny = seq // nx
    rows = [[y * nx + x for x in range(nx)] for y in range(ny)]
    columns = [[y * nx + x for y in range(ny)] for x in range(nx)]

    def along_x(step):
        return [(y * nx + x, y * nx + (x + step) % nx) for y in range(ny) for x in range(nx)]

    right, left = along_x(1), along_x(-1)
    tokens = inputs_saved.shape[3]
    width = inputs_saved.shape[4]
    channels = grad_latent.shape[-1]
    piece = grad_latent.shape[3]

    both = lax.all_gather(grad_latent[0, 0][:, None], "seq", axis=1, tiled=True, axis_index_groups=columns)
    rev = lax.all_gather(both[1][:, None], "seq", axis=1, tiled=True, axis_index_groups=rows)
    rev = rev.reshape(tokens, channels)

    own = both[0]
    half = ny // 2
    from_left, from_right = [own], [own]
    for _ in range(nx // 2 - 1):
        from_left.append(lax.ppermute(from_left[-1], "seq", right))
        from_right.append(lax.ppermute(from_right[-1], "seq", left))
    far = jnp.concatenate(
        [
            lax.ppermute(from_left[-1][:half], "seq", right),
            lax.ppermute(from_right[-1][half:], "seq", left),
        ]
    )
    x_here = lax.rem(lax.axis_index("seq"), nx)
    relative = from_right + [far] + from_left[:0:-1]
    fwd = jnp.zeros((ny, nx, piece, channels), own.dtype)
    for k, block in enumerate(relative):
        fwd = lax.dynamic_update_slice(fwd, block[:, None], (0, lax.rem(x_here + k, nx), 0, 0))
    fwd = fwd.reshape(tokens, channels)

    over_tokens = (((0,), (0,)), ((), ()))

    def dp_sum(latent, saved):
        partial = lax.dot_general(latent, saved, over_tokens, preferred_element_type=jnp.float32)
        shares = partial.astype(jnp.bfloat16).reshape(dp, channels // dp, width)
        shares = lax.all_to_all(shares, "dp", 0, 0, tiled=True)
        return jnp.sum(shares.astype(jnp.float32), axis=0)

    sum_rev = dp_sum(rev, inputs_saved[0, 0, 1])
    mirrored = lax.ppermute(sum_rev.astype(jnp.bfloat16), "pipe", [(i, pipe - 1 - i) for i in range(pipe)])
    sum_fwd = dp_sum(fwd, inputs_saved[0, 0, 0])
    input_grad = lax.dot_general(
        fwd, weights[0], (((1,), (1,)), ((), ())), preferred_element_type=jnp.float32
    ).astype(jnp.bfloat16)
    weight_grad = (sum_fwd + mirrored.astype(jnp.float32)) * (1.0 / tokens)
    return input_grad[None, None], weight_grad.T[None]


def solution(mesh):
    in_specs = (
        P("pipe", "dp", None, None, "seq"),
        P("pipe", "dp", None, "seq", None),
        P("pipe", "seq", None),
    )
    out_specs = (P("pipe", "dp", None, "seq"), P("pipe", "seq", "dp"))
    return jax.shard_map(local, mesh=mesh, in_specs=in_specs, out_specs=out_specs, check_vma=False)
```

```python
import jax
import jax.numpy as jnp
from jax import lax
from jax.experimental import pallas as pl
from jax.experimental.pallas import tpu as pltpu
from jax.sharding import PartitionSpec as P

X_CHIPS = 8
VMEM_BYTES = 40 * 2**20


def partials_kernel(x_ref, *refs):
    blocks, (saved_ref, shares_ref, latent_ref, rev_ref) = refs[:-4], refs[-4:]
    nx = latent_ref.shape[1]
    far = nx // 2
    held = (latent_ref, rev_ref)
    for k in range(nx):
        place = lax.rem(x_ref[0] + k, nx)
        for direction in range(2):
            if k == far:
                block = blocks[k + direction]
                for y in range(latent_ref.shape[0]):
                    held[direction][y, place] = block[y]
            else:
                block = blocks[k if k < far else k + 1]
                for y in range(latent_ref.shape[0]):
                    held[direction][y, place] = block[direction, y]
    dp, _, share, _ = shares_ref.shape
    for direction in range(2):
        latent = held[direction][...].reshape(-1, dp * share)
        partial = jnp.dot(saved_ref[direction], latent, preferred_element_type=jnp.float32)
        turned = partial.T.astype(shares_ref.dtype)
        for part in range(dp):
            shares_ref[part, direction] = turned[part * share : (part + 1) * share]


def local(inputs_saved, grad_latent, weights):
    seq = lax.axis_size("seq")
    pipe = lax.axis_size("pipe")
    dp = lax.axis_size("dp")
    nx = X_CHIPS
    ny = seq // nx
    columns = [[y * nx + x for y in range(ny)] for x in range(nx)]

    def along_x(step):
        return [(y * nx + x, y * nx + (x + step) % nx) for y in range(ny) for x in range(nx)]

    right, left = along_x(1), along_x(-1)
    tokens = inputs_saved.shape[3]
    width = inputs_saved.shape[4]
    channels = grad_latent.shape[-1]
    piece = grad_latent.shape[3]

    both = lax.all_gather(grad_latent[0, 0][:, None], "seq", axis=1, tiled=True, axis_index_groups=columns)
    own = both
    from_left, from_right = [own], [own]
    for _ in range(nx // 2 - 1):
        from_left.append(lax.ppermute(from_left[-1], "seq", right))
        from_right.append(lax.ppermute(from_right[-1], "seq", left))
    far_fwd = lax.ppermute(from_left[-1][0], "seq", right)
    far_rev = lax.ppermute(from_right[-1][1], "seq", left)
    blocks = from_right + [far_fwd, far_rev] + from_left[:0:-1]
    x_here = lax.rem(lax.axis_index("seq"), nx).reshape(1)
    vmem = pl.BlockSpec(memory_space=pltpu.VMEM)
    shares, latent_fwd = pl.pallas_call(
        partials_kernel,
        out_shape=(
            jax.ShapeDtypeStruct((dp, 2, channels // dp, width), jnp.bfloat16),
            jax.ShapeDtypeStruct((ny, nx, piece, channels), own.dtype),
        ),
        in_specs=[pl.BlockSpec(memory_space=pltpu.SMEM)] + [vmem] * (len(blocks) + 1),
        out_specs=(vmem, vmem),
        scratch_shapes=[pltpu.VMEM((ny, nx, piece, channels), own.dtype)],
        compiler_params=pltpu.CompilerParams(vmem_limit_bytes=VMEM_BYTES),
        cost_estimate=pl.CostEstimate(
            flops=4 * tokens * channels * width,
            bytes_accessed=4 * tokens * (width + channels),
            transcendentals=0,
        ),
    )(x_here, *blocks, jnp.swapaxes(inputs_saved[0, 0], 1, 2))

    shares = lax.all_to_all(shares, "dp", 0, 0, tiled=True).astype(jnp.float32)
    sum_rev = jnp.sum(shares[:, 1], axis=0)
    mirrored = lax.ppermute(
        sum_rev.astype(jnp.bfloat16), "pipe", [(i, pipe - 1 - i) for i in range(pipe)]
    )
    sum_fwd = jnp.sum(shares[:, 0], axis=0)
    input_grad = lax.dot_general(
        latent_fwd.reshape(tokens, channels),
        weights[0],
        (((1,), (1,)), ((), ())),
        preferred_element_type=jnp.float32,
    ).astype(jnp.bfloat16)
    weight_grad = (sum_fwd + mirrored.astype(jnp.float32)) * (1.0 / tokens)
    return input_grad[None, None], weight_grad.T[None]


def solution(mesh):
    in_specs = (
        P("pipe", "dp", None, None, "seq"),
        P("pipe", "dp", None, "seq", None),
        P("pipe", "seq", None),
    )
    out_specs = (P("pipe", "dp", None, "seq"), P("pipe", "seq", "dp"))
    return jax.shard_map(local, mesh=mesh, in_specs=in_specs, out_specs=out_specs, check_vma=False)
```

```python
import jax
import jax.numpy as jnp
from jax import lax
from jax.experimental import pallas as pl
from jax.experimental.pallas import tpu as pltpu
from jax.sharding import PartitionSpec as P

X_CHIPS = 8
VMEM_BYTES = 40 * 2**20


def partials_kernel(place_ref, *refs):
    pieces, (fwd_ref, rev_ref, shares_ref, latent_ref, held_ref) = refs[:-5], refs[-5:]
    ny, nx = latent_ref.shape[:2]
    far, blocks = pieces[:2], pieces[2:]
    half = ny // 2
    dp, _, share, _ = shares_ref.shape
    for direction, (target, saved_ref) in enumerate(((latent_ref, fwd_ref), (held_ref, rev_ref))):
        for y in range(ny):
            target[y, place_ref[0]] = far[y // half][y % half, direction]
            for k, block in enumerate(blocks):
                target[y, place_ref[k + 1]] = block[y, direction]
        latent = target[...].reshape(-1, dp * share)
        partial = jnp.dot(saved_ref[...], latent, preferred_element_type=jnp.float32)
        turned = partial.T.astype(shares_ref.dtype)
        for part in range(dp):
            shares_ref[part, direction] = turned[part * share : (part + 1) * share]


def local(inputs_saved, grad_latent, weights):
    seq = lax.axis_size("seq")
    pipe = lax.axis_size("pipe")
    dp = lax.axis_size("dp")
    nx = X_CHIPS
    ny = seq // nx
    columns = [[y * nx + x for y in range(ny)] for x in range(nx)]

    def along_x(step):
        return [
            (
                (y * nx + x) * dp + d,
                (y * nx + (x + (step if d % 2 == 0 else -step)) % nx) * dp + d,
            )
            for y in range(ny)
            for x in range(nx)
            for d in range(dp)
        ]

    ahead, back = along_x(1), along_x(-1)
    tokens = inputs_saved.shape[3]
    width = inputs_saved.shape[4]
    channels = grad_latent.shape[-1]
    piece = grad_latent.shape[3]

    own = lax.all_gather(grad_latent[0, 0], "seq", axis=0, tiled=True, axis_index_groups=columns)
    own = own.reshape(ny, 2, piece, channels)
    half = ny // 2
    first, second = [own], [own]
    for _ in range(nx // 2 - 1):
        first.append(lax.ppermute(first[-1], ("seq", "dp"), ahead))
        second.append(lax.ppermute(second[-1], ("seq", "dp"), back))
    blocks = [
        lax.ppermute(first[-1][:half], ("seq", "dp"), ahead),
        lax.ppermute(second[-1][half:], ("seq", "dp"), back),
    ]
    x_here = lax.rem(lax.axis_index("seq"), nx)
    sign = 1 - 2 * lax.rem(lax.axis_index("dp"), 2)
    blocks += first + second[1:]
    steps = [nx // 2] + [-k for k in range(len(first))] + list(range(1, len(second)))
    places = jnp.stack([lax.rem(x_here + nx + sign * step, nx) for step in steps])
    saved_fwd, saved_rev = inputs_saved[0, 0, 0].T, inputs_saved[0, 0, 1].T
    vmem = pl.BlockSpec(memory_space=pltpu.VMEM)
    shares, latent_fwd = pl.pallas_call(
        partials_kernel,
        out_shape=(
            jax.ShapeDtypeStruct((dp, 2, channels // dp, width), jnp.bfloat16),
            jax.ShapeDtypeStruct((ny, nx, piece, channels), own.dtype),
        ),
        in_specs=[pl.BlockSpec(memory_space=pltpu.SMEM)] + [vmem] * (len(blocks) + 2),
        out_specs=(vmem, vmem),
        scratch_shapes=[pltpu.VMEM((ny, nx, piece, channels), own.dtype)],
        compiler_params=pltpu.CompilerParams(vmem_limit_bytes=VMEM_BYTES),
        cost_estimate=pl.CostEstimate(
            flops=4 * tokens * channels * width,
            bytes_accessed=4 * tokens * (width + channels),
            transcendentals=0,
        ),
    )(places, *blocks, saved_fwd, saved_rev)

    shares = lax.all_to_all(shares, "dp", 0, 0, tiled=True).astype(jnp.float32)
    sum_rev = jnp.sum(shares[:, 1], axis=0)
    mirrored = lax.ppermute(
        sum_rev.astype(jnp.bfloat16), "pipe", [(i, pipe - 1 - i) for i in range(pipe)]
    )
    sum_fwd = jnp.sum(shares[:, 0], axis=0)
    input_grad = lax.dot_general(
        latent_fwd.reshape(tokens, channels),
        weights[0],
        (((1,), (1,)), ((), ())),
        preferred_element_type=jnp.float32,
    ).astype(jnp.bfloat16)
    weight_grad = (sum_fwd + mirrored.astype(jnp.float32)) * (1.0 / tokens)
    return input_grad[None, None], weight_grad.T[None]


def solution(mesh):
    in_specs = (
        P("pipe", "dp", None, None, "seq"),
        P("pipe", "dp", None, "seq", None),
        P("pipe", "seq", None),
    )
    out_specs = (P("pipe", "dp", None, "seq"), P("pipe", "seq", "dp"))
    return jax.shard_map(local, mesh=mesh, in_specs=in_specs, out_specs=out_specs, check_vma=False)
```

```python
import jax
import jax.numpy as jnp
from jax import lax
from jax.experimental import pallas as pl
from jax.experimental.pallas import tpu as pltpu
from jax.sharding import PartitionSpec as P

X_CHIPS = 8
VMEM_BYTES = 40 * 2**20


def early_kernel(x_ref, *refs):
    blocks, (saved_ref, partial_ref, picked_ref, latent_ref, rev_ref) = refs[:-5], refs[-5:]
    ny, nx, piece, channels = latent_ref.shape
    far = nx // 2
    width = saved_ref.shape[1]
    far_place = lax.rem(x_ref[0] + far, nx)
    row = lax.broadcasted_iota(jnp.int32, (nx * piece, piece), 0)
    column = lax.broadcasted_iota(jnp.int32, (nx * piece, piece), 1)
    pick = jnp.where(row == column + far_place * piece, 1.0, 0.0).astype(saved_ref.dtype)
    for direction, target in enumerate((latent_ref, rev_ref)):
        for k, block in enumerate(blocks):
            place = lax.rem(x_ref[0] + (k if k < far else k + 1), nx)
            for y in range(ny):
                target[y, place] = block[direction, y]
        for y in range(ny):
            target[y, far_place] = jnp.zeros((piece, channels), target.dtype)
            part = saved_ref[direction, :, y * nx * piece : (y + 1) * nx * piece]
            picked = jnp.dot(part, pick, preferred_element_type=jnp.float32)
            picked_ref[direction, y] = picked.astype(picked_ref.dtype)
        latent = target[...].reshape(-1, channels)
        partial_ref[direction] = jnp.dot(
            saved_ref[direction], latent, preferred_element_type=jnp.float32
        )


def late_kernel(x_ref, fwd_ref, rev_ref, partial_ref, picked_ref, latent_in, *refs):
    shares_ref, latent_ref, sem = refs
    ny, nx = latent_in.shape[:2]
    dp, _, share, _ = shares_ref.shape
    far_place = lax.rem(x_ref[0] + nx // 2, nx)
    fill = pltpu.make_async_copy(fwd_ref, latent_ref.at[:, far_place], sem)
    fill.start()
    for direction, far_ref in enumerate((fwd_ref, rev_ref)):
        total = partial_ref[direction]
        for y in range(ny):
            total += jnp.dot(
                picked_ref[direction, y], far_ref[y], preferred_element_type=jnp.float32
            )
        turned = total.T.astype(shares_ref.dtype)
        for part in range(dp):
            shares_ref[part, direction] = turned[part * share : (part + 1) * share]
    fill.wait()


def local(inputs_saved, grad_latent, weights):
    seq = lax.axis_size("seq")
    pipe = lax.axis_size("pipe")
    dp = lax.axis_size("dp")
    nx = X_CHIPS
    ny = seq // nx
    columns = [[y * nx + x for y in range(ny)] for x in range(nx)]

    def along_x(step):
        return [(y * nx + x, y * nx + (x + step) % nx) for y in range(ny) for x in range(nx)]

    right, left = along_x(1), along_x(-1)
    tokens = inputs_saved.shape[3]
    width = inputs_saved.shape[4]
    channels = grad_latent.shape[-1]
    piece = grad_latent.shape[3]

    both = lax.all_gather(grad_latent[0, 0][:, None], "seq", axis=1, tiled=True, axis_index_groups=columns)
    own = both
    from_left, from_right = [own], [own]
    for _ in range(nx // 2 - 1):
        from_left.append(lax.ppermute(from_left[-1], "seq", right))
        from_right.append(lax.ppermute(from_right[-1], "seq", left))
    far_fwd = lax.ppermute(from_left[-1][0], "seq", right)
    far_rev = lax.ppermute(from_right[-1][1], "seq", left)
    blocks = from_right + from_left[:0:-1]
    x_here = lax.rem(lax.axis_index("seq"), nx).reshape(1)
    saved = jnp.swapaxes(inputs_saved[0, 0], 1, 2)
    vmem = pl.BlockSpec(memory_space=pltpu.VMEM)
    smem = pl.BlockSpec(memory_space=pltpu.SMEM)
    anywhere = pl.BlockSpec(memory_space=pl.ANY)
    latent_shape = jax.ShapeDtypeStruct((ny, nx, piece, channels), own.dtype)
    settings = pltpu.CompilerParams(vmem_limit_bytes=VMEM_BYTES)
    partial, picked, latent_fwd = pl.pallas_call(
        early_kernel,
        out_shape=(
            jax.ShapeDtypeStruct((2, width, channels), jnp.float32),
            jax.ShapeDtypeStruct((2, ny, width, piece), saved.dtype),
            latent_shape,
        ),
        in_specs=[smem] + [vmem] * (len(blocks) + 1),
        out_specs=(vmem, vmem, vmem),
        scratch_shapes=[pltpu.VMEM(latent_shape.shape, own.dtype)],
        compiler_params=settings,
        cost_estimate=pl.CostEstimate(
            flops=4 * tokens * channels * width,
            bytes_accessed=4 * tokens * (width + channels),
            transcendentals=0,
        ),
    )(x_here, *blocks, saved)
    shares, latent_fwd = pl.pallas_call(
        late_kernel,
        out_shape=(
            jax.ShapeDtypeStruct((dp, 2, channels // dp, width), jnp.bfloat16),
            latent_shape,
        ),
        in_specs=[smem] + [vmem] * 4 + [anywhere],
        out_specs=(vmem, anywhere),
        scratch_shapes=[pltpu.SemaphoreType.DMA],
        input_output_aliases={5: 1},
        compiler_params=settings,
        cost_estimate=pl.CostEstimate(
            flops=4 * ny * piece * channels * width,
            bytes_accessed=12 * channels * width,
            transcendentals=0,
        ),
    )(x_here, far_fwd, far_rev, partial, picked, latent_fwd)

    shares = lax.all_to_all(shares, "dp", 0, 0, tiled=True).astype(jnp.float32)
    sum_rev = jnp.sum(shares[:, 1], axis=0)
    mirrored = lax.ppermute(
        sum_rev.astype(jnp.bfloat16), "pipe", [(i, pipe - 1 - i) for i in range(pipe)]
    )
    sum_fwd = jnp.sum(shares[:, 0], axis=0)
    input_grad = lax.dot_general(
        latent_fwd.reshape(tokens, channels),
        weights[0],
        (((1,), (1,)), ((), ())),
        preferred_element_type=jnp.float32,
    ).astype(jnp.bfloat16)
    weight_grad = (sum_fwd + mirrored.astype(jnp.float32)) * (1.0 / tokens)
    return input_grad[None, None], weight_grad.T[None]


def solution(mesh):
    in_specs = (
        P("pipe", "dp", None, None, "seq"),
        P("pipe", "dp", None, "seq", None),
        P("pipe", "seq", None),
    )
    out_specs = (P("pipe", "dp", None, "seq"), P("pipe", "seq", "dp"))
    return jax.shard_map(local, mesh=mesh, in_specs=in_specs, out_specs=out_specs, check_vma=False)
```

```python
import jax
import jax.numpy as jnp
from jax import lax
from jax.experimental import pallas as pl
from jax.experimental.pallas import tpu as pltpu
from jax.sharding import PartitionSpec as P

X_CHIPS = 8
VMEM_BYTES = 40 * 2**20


ROWS_BY_ROWS = (((1,), (1,)), ((), ()))


def early_kernel(here_ref, *refs):
    blocks, refs = refs[:-7], refs[-7:]
    saved_ref, weight_ref, partial_ref, picked_ref, grad_ref, latent_ref, rev_ref = refs
    ny, nx, piece, channels = latent_ref.shape
    far = nx // 2
    far_place = lax.rem(here_ref[0] + far, nx)
    row = lax.broadcasted_iota(jnp.int32, (nx * piece, piece), 0)
    column = lax.broadcasted_iota(jnp.int32, (nx * piece, piece), 1)
    pick = jnp.where(row == column + far_place * piece, 1.0, 0.0).astype(saved_ref.dtype)
    for direction, target in enumerate((latent_ref, rev_ref)):
        for k, block in enumerate(blocks):
            place = lax.rem(here_ref[0] + (k if k < far else k + 1), nx)
            for y in range(ny):
                target[y, place] = block[direction, y]
        for y in range(ny):
            target[y, far_place] = jnp.zeros((piece, channels), target.dtype)
            part = saved_ref[direction, :, y * nx * piece : (y + 1) * nx * piece]
            picked = jnp.dot(part, pick, preferred_element_type=jnp.float32)
            picked_ref[direction, y] = picked.astype(picked_ref.dtype)
        latent = target[...].reshape(-1, channels)
        partial_ref[direction] = jnp.dot(
            saved_ref[direction], latent, preferred_element_type=jnp.float32
        )
        if direction == 0:
            grad = lax.dot_general(
                weight_ref[...], latent, ROWS_BY_ROWS, preferred_element_type=jnp.float32
            )
            grad_ref[...] = grad.astype(grad_ref.dtype)


def late_kernel(here_ref, fwd_ref, rev_ref, *refs):
    weight_ref, partial_ref, picked_ref, early_ref, shares_ref, grad_ref = refs
    _, dp, share, _ = shares_ref.shape
    ny, piece, channels = fwd_ref.shape
    run = early_ref.shape[1] // ny
    nx = run // piece
    far_place = lax.rem(here_ref[0] + nx // 2, nx)
    for direction, far_ref in enumerate((fwd_ref, rev_ref)):
        total = partial_ref[direction]
        for y in range(ny):
            total += jnp.dot(
                picked_ref[direction, y], far_ref[y], preferred_element_type=jnp.float32
            )
        turned = total.T.astype(shares_ref.dtype)
        slot = lax.rem(here_ref[1] + direction, 2)
        for part in range(dp):
            shares_ref[slot, part] = turned[part * share : (part + 1) * share]
    row = lax.broadcasted_iota(jnp.int32, (piece, run), 0)
    column = lax.broadcasted_iota(jnp.int32, (piece, run), 1)
    put = jnp.where(column == row + far_place * piece, 1.0, 0.0).astype(grad_ref.dtype)
    for y in range(ny):
        grad = lax.dot_general(
            weight_ref[...], fwd_ref[y], ROWS_BY_ROWS, preferred_element_type=jnp.float32
        )
        spread = jnp.dot(grad.astype(grad_ref.dtype), put, preferred_element_type=jnp.float32)
        lanes = slice(y * run, (y + 1) * run)
        grad_ref[:, lanes] = early_ref[:, lanes] + spread.astype(grad_ref.dtype)


def local(inputs_saved, grad_latent, weights):
    seq = lax.axis_size("seq")
    pipe = lax.axis_size("pipe")
    dp = lax.axis_size("dp")
    nx = X_CHIPS
    ny = seq // nx
    columns = [[y * nx + x for y in range(ny)] for x in range(nx)]

    def along_x(step):
        return [(y * nx + x, y * nx + (x + step) % nx) for y in range(ny) for x in range(nx)]

    right, left = along_x(1), along_x(-1)
    tokens = inputs_saved.shape[3]
    width = inputs_saved.shape[4]
    channels = grad_latent.shape[-1]
    piece = grad_latent.shape[3]

    both = lax.all_gather(grad_latent[0, 0][:, None], "seq", axis=1, tiled=True, axis_index_groups=columns)
    own = both
    from_left, from_right = [own], [own]
    for _ in range(nx // 2 - 1):
        from_left.append(lax.ppermute(from_left[-1], "seq", right))
        from_right.append(lax.ppermute(from_right[-1], "seq", left))
    far_fwd = lax.ppermute(from_left[-1][0], "seq", right)
    far_rev = lax.ppermute(from_right[-1][1], "seq", left)
    blocks = from_right + from_left[:0:-1]
    here = jnp.stack(
        [lax.rem(lax.axis_index("seq"), nx), lax.div(lax.axis_index("pipe"), pipe // 2)]
    )
    saved = jnp.swapaxes(inputs_saved[0, 0], 1, 2)
    vmem = pl.BlockSpec(memory_space=pltpu.VMEM)
    smem = pl.BlockSpec(memory_space=pltpu.SMEM)
    held = pltpu.VMEM((ny, nx, piece, channels), own.dtype)
    grad_shape = jax.ShapeDtypeStruct((width, tokens), own.dtype)
    settings = pltpu.CompilerParams(vmem_limit_bytes=VMEM_BYTES)
    partial, picked, grad = pl.pallas_call(
        early_kernel,
        out_shape=(
            jax.ShapeDtypeStruct((2, width, channels), jnp.float32),
            jax.ShapeDtypeStruct((2, ny, width, piece), saved.dtype),
            grad_shape,
        ),
        in_specs=[smem] + [vmem] * (len(blocks) + 2),
        out_specs=(vmem, vmem, vmem),
        scratch_shapes=[held, held],
        compiler_params=settings,
        cost_estimate=pl.CostEstimate(
            flops=6 * tokens * channels * width,
            bytes_accessed=4 * tokens * (width + channels),
            transcendentals=0,
        ),
    )(here, *blocks, saved, weights[0])
    shares, grad = pl.pallas_call(
        late_kernel,
        out_shape=(
            jax.ShapeDtypeStruct((2, dp, channels // dp, width), jnp.bfloat16),
            grad_shape,
        ),
        in_specs=[smem] + [vmem] * 6,
        out_specs=(vmem, vmem),
        compiler_params=settings,
        cost_estimate=pl.CostEstimate(
            flops=6 * ny * piece * channels * width,
            bytes_accessed=12 * channels * width,
            transcendentals=0,
        ),
    )(here, far_fwd, far_rev, weights[0], partial, picked, grad)

    ends = [[p * dp + d for p in (i, pipe - 1 - i) for d in range(dp)] for i in range(pipe // 2)]
    shares = lax.all_to_all(
        shares.reshape(2 * dp, channels // dp, width),
        ("pipe", "dp"),
        0,
        0,
        tiled=True,
        axis_index_groups=ends,
    )
    weight_grad = jnp.sum(shares.astype(jnp.float32), axis=0) * (1.0 / tokens)
    return grad.T[None, None], weight_grad.T[None]


def solution(mesh):
    in_specs = (
        P("pipe", "dp", None, None, "seq"),
        P("pipe", "dp", None, "seq", None),
        P("pipe", "seq", None),
    )
    out_specs = (P("pipe", "dp", None, "seq"), P("pipe", "seq", "dp"))
    return jax.shard_map(local, mesh=mesh, in_specs=in_specs, out_specs=out_specs, check_vma=False)
```

```python
import jax
import jax.numpy as jnp
from jax import lax
from jax.experimental import pallas as pl
from jax.experimental.pallas import tpu as pltpu
from jax.sharding import PartitionSpec as P

X_CHIPS = 8
VMEM_BYTES = 40 * 2**20


def near_steps(nx):
    far = nx // 2
    return list(range(far - 1)) + [nx - k for k in range(1, far - 1)]


def late_steps(nx):
    return nx // 2 - 1, nx // 2 + 1, nx // 2


def early_kernel(here_ref, *refs):
    blocks, (saved_ref, partial_ref, picked_ref, latent_ref) = refs[:-4], refs[-4:]
    ny, nx, piece, channels = latent_ref.shape
    run = nx * piece
    row = lax.broadcasted_iota(jnp.int32, (run, piece), 0)
    column = lax.broadcasted_iota(jnp.int32, (run, piece), 1)
    nothing = jnp.zeros((piece, channels), latent_ref.dtype)
    for direction in range(2):
        for step, block in zip(near_steps(nx), blocks):
            place = lax.rem(here_ref[0] + step, nx)
            for y in range(ny):
                latent_ref[y, place] = block[direction, y]
        for j, step in enumerate(late_steps(nx)):
            place = lax.rem(here_ref[0] + step, nx)
            pick = jnp.where(row == column + place * piece, 1.0, 0.0).astype(saved_ref.dtype)
            for y in range(ny):
                latent_ref[y, place] = nothing
                part = saved_ref[direction, :, y * run : (y + 1) * run]
                picked = jnp.dot(part, pick, preferred_element_type=jnp.float32)
                picked_ref[direction, j, y] = picked.astype(picked_ref.dtype)
        partial_ref[direction] = jnp.dot(
            saved_ref[direction],
            latent_ref[...].reshape(-1, channels),
            preferred_element_type=jnp.float32,
        )


def put_shares(total, shares, slot):
    dp, share, _ = shares.shape[1:]
    turned = total.T.astype(shares.dtype)
    for part in range(dp):
        shares[slot, part] = turned[part * share : (part + 1) * share]


def middle_kernel(here_ref, *refs):
    blocks, refs = refs[:-8], refs[-8:]
    far_ref, weight_ref, partial_ref, picked_ref, fwd_ref, rev_ref, grad_ref, latent_ref = refs
    ny, nx, _, channels = latent_ref.shape
    late = blocks[-2:]
    for step, block in zip(near_steps(nx) + list(late_steps(nx)[:2]), blocks):
        place = lax.rem(here_ref[0] + step, nx)
        for y in range(ny):
            latent_ref[y, place] = block[0, y]
    place = lax.rem(here_ref[0] + late_steps(nx)[2], nx)
    for y in range(ny):
        latent_ref[y, place] = far_ref[y]
    grad = lax.dot_general(
        weight_ref[...],
        latent_ref[...].reshape(-1, channels),
        (((1,), (1,)), ((), ())),
        preferred_element_type=jnp.float32,
    )
    grad_ref[...] = grad.astype(grad_ref.dtype)
    for direction in range(2):
        total = partial_ref[direction]
        for y in range(ny):
            for j, block in enumerate(late):
                total += jnp.dot(
                    picked_ref[direction, j, y],
                    block[direction, y],
                    preferred_element_type=jnp.float32,
                )
            if direction == 0:
                total += jnp.dot(
                    picked_ref[0, 2, y], far_ref[y], preferred_element_type=jnp.float32
                )
        if direction == 0:
            put_shares(total, fwd_ref, 0)
        else:
            rev_ref[...] = total


def late_kernel(here_ref, far_ref, rev_ref, picked_ref, fwd_ref, shares_ref):
    total = rev_ref[...]
    for y in range(far_ref.shape[0]):
        total += jnp.dot(picked_ref[1, 2, y], far_ref[y], preferred_element_type=jnp.float32)
    put_shares(total, shares_ref, 1 - here_ref[1])
    shares_ref[here_ref[1]] = fwd_ref[0]


def local(inputs_saved, grad_latent, weights):
    seq = lax.axis_size("seq")
    pipe = lax.axis_size("pipe")
    dp = lax.axis_size("dp")
    nx = X_CHIPS
    ny = seq // nx
    columns = [[y * nx + x for y in range(ny)] for x in range(nx)]

    def along_x(step):
        return [(y * nx + x, y * nx + (x + step) % nx) for y in range(ny) for x in range(nx)]

    right, left = along_x(1), along_x(-1)
    tokens = inputs_saved.shape[3]
    width = inputs_saved.shape[4]
    channels = grad_latent.shape[-1]
    piece = grad_latent.shape[3]

    both = lax.all_gather(grad_latent[0, 0][:, None], "seq", axis=1, tiled=True, axis_index_groups=columns)
    own = both
    from_left, from_right = [own], [own]
    for _ in range(nx // 2 - 1):
        from_left.append(lax.ppermute(from_left[-1], "seq", right))
        from_right.append(lax.ppermute(from_right[-1], "seq", left))
    far = nx // 2
    near = from_right[: far - 1] + from_left[1 : far - 1]
    here = jnp.stack(
        [lax.rem(lax.axis_index("seq"), nx), lax.div(lax.axis_index("pipe"), pipe // 2)]
    )
    saved = jnp.swapaxes(inputs_saved[0, 0], 1, 2)
    vmem = pl.BlockSpec(memory_space=pltpu.VMEM)
    smem = pl.BlockSpec(memory_space=pltpu.SMEM)
    held = pltpu.VMEM((ny, nx, piece, channels), own.dtype)
    settings = pltpu.CompilerParams(vmem_limit_bytes=VMEM_BYTES)

    def kernel_call(body, out_shape, scratch, flops, *operands):
        return pl.pallas_call(
            body,
            out_shape=out_shape,
            in_specs=[smem] + [vmem] * len(operands),
            out_specs=(vmem,) * len(out_shape),
            scratch_shapes=scratch,
            compiler_params=settings,
            cost_estimate=pl.CostEstimate(
                flops=flops, bytes_accessed=4 * tokens * channels, transcendentals=0
            ),
        )(here, *operands)

    product = 2 * tokens * channels * width
    partial, picked = kernel_call(
        early_kernel,
        (
            jax.ShapeDtypeStruct((2, width, channels), jnp.float32),
            jax.ShapeDtypeStruct((2, 3, ny, width, piece), saved.dtype),
        ),
        [held],
        2 * product,
        *near,
        saved,
    )
    last_left, partial = lax.optimization_barrier((from_left[-1], partial))
    far_fwd = lax.ppermute(last_left[0], "seq", right)
    far_rev = lax.ppermute(from_right[-1][1], "seq", left)
    share_shape = (dp, channels // dp, width)
    shares_fwd, total_rev, grad = kernel_call(
        middle_kernel,
        (
            jax.ShapeDtypeStruct((1,) + share_shape, jnp.bfloat16),
            jax.ShapeDtypeStruct((width, channels), jnp.float32),
            jax.ShapeDtypeStruct((width, tokens), own.dtype),
        ),
        [held],
        2 * product,
        *near,
        from_right[-1],
        last_left,
        far_fwd,
        weights[0],
        partial,
        picked,
    )
    (shares,) = kernel_call(
        late_kernel,
        (jax.ShapeDtypeStruct((2,) + share_shape, jnp.bfloat16),),
        [],
        product // 8,
        far_rev,
        total_rev,
        picked,
        shares_fwd,
    )

    ends = [[p * dp + d for p in (i, pipe - 1 - i) for d in range(dp)] for i in range(pipe // 2)]
    shares = lax.all_to_all(
        shares.reshape(2 * dp, channels // dp, width),
        ("pipe", "dp"),
        0,
        0,
        tiled=True,
        axis_index_groups=ends,
    )
    weight_grad = jnp.sum(shares.astype(jnp.float32), axis=0) * (1.0 / tokens)
    return grad.T[None, None], weight_grad.T[None]


def solution(mesh):
    in_specs = (
        P("pipe", "dp", None, None, "seq"),
        P("pipe", "dp", None, "seq", None),
        P("pipe", "seq", None),
    )
    out_specs = (P("pipe", "dp", None, "seq"), P("pipe", "seq", "dp"))
    return jax.shard_map(local, mesh=mesh, in_specs=in_specs, out_specs=out_specs, check_vma=False)
```

```python
import jax
import jax.numpy as jnp
from jax import lax
from jax.experimental import pallas as pl
from jax.experimental.pallas import tpu as pltpu
from jax.sharding import PartitionSpec as P

X_CHIPS = 8
VMEM_BYTES = 40 * 2**20


def near_steps(nx):
    far = nx // 2
    return list(range(far - 1)) + [nx - k for k in range(1, far - 1)]


def late_steps(nx):
    return nx // 2 - 1, nx // 2 + 1, nx // 2


def early_kernel(here_ref, *refs):
    blocks, (saved_ref, partial_ref, picked_ref, latent_ref) = refs[:-4], refs[-4:]
    ny, nx, piece, channels = latent_ref.shape
    run = nx * piece
    row = lax.broadcasted_iota(jnp.int32, (run, piece), 0)
    column = lax.broadcasted_iota(jnp.int32, (run, piece), 1)
    nothing = jnp.zeros((piece, channels), latent_ref.dtype)
    for direction in range(2):
        for step, block in zip(near_steps(nx), blocks):
            place = lax.rem(here_ref[0] + step, nx)
            for y in range(ny):
                latent_ref[y, place] = block[direction, y]
        for j, step in enumerate(late_steps(nx)):
            place = lax.rem(here_ref[0] + step, nx)
            pick = jnp.where(row == column + place * piece, 1.0, 0.0).astype(saved_ref.dtype)
            for y in range(ny):
                latent_ref[y, place] = nothing
                part = saved_ref[direction, :, y * run : (y + 1) * run]
                picked = jnp.dot(part, pick, preferred_element_type=jnp.float32)
                picked_ref[direction, j, y] = picked.astype(picked_ref.dtype)
        partial_ref[direction] = jnp.dot(
            saved_ref[direction],
            latent_ref[...].reshape(-1, channels),
            preferred_element_type=jnp.float32,
        )


def third_kernel(here_ref, low_ref, high_ref, partial_ref, picked_ref, total_ref):
    for direction in range(2):
        total = partial_ref[direction]
        for j, block in enumerate((low_ref, high_ref)):
            for y in range(block.shape[1]):
                total += jnp.dot(
                    picked_ref[direction, j, y],
                    block[direction, y],
                    preferred_element_type=jnp.float32,
                )
        total_ref[direction] = total


def put_shares(total, shares, slot):
    dp, share, _ = shares.shape[1:]
    turned = total.T.astype(shares.dtype)
    for part in range(dp):
        shares[slot, part] = turned[part * share : (part + 1) * share]


def middle_kernel(here_ref, *refs):
    blocks, refs = refs[:-7], refs[-7:]
    far_ref, weight_ref, partial_ref, picked_ref, fwd_ref, grad_ref, latent_ref = refs
    ny, nx, _, channels = latent_ref.shape
    for step, block in zip(near_steps(nx) + list(late_steps(nx)[:2]), blocks):
        place = lax.rem(here_ref[0] + step, nx)
        for y in range(ny):
            latent_ref[y, place] = block[0, y]
    place = lax.rem(here_ref[0] + late_steps(nx)[2], nx)
    total = partial_ref[0]
    for y in range(ny):
        latent_ref[y, place] = far_ref[y]
        total += jnp.dot(picked_ref[0, 2, y], far_ref[y], preferred_element_type=jnp.float32)
    put_shares(total, fwd_ref, 0)
    grad = lax.dot_general(
        weight_ref[...],
        latent_ref[...].reshape(-1, channels),
        (((1,), (1,)), ((), ())),
        preferred_element_type=jnp.float32,
    )
    grad_ref[...] = grad.astype(grad_ref.dtype)


def late_kernel(here_ref, far_ref, partial_ref, picked_ref, fwd_ref, shares_ref):
    total = partial_ref[1]
    for y in range(far_ref.shape[0]):
        total += jnp.dot(picked_ref[1, 2, y], far_ref[y], preferred_element_type=jnp.float32)
    put_shares(total, shares_ref, 1 - here_ref[1])
    shares_ref[here_ref[1]] = fwd_ref[0]


def local(inputs_saved, grad_latent, weights):
    seq = lax.axis_size("seq")
    pipe = lax.axis_size("pipe")
    dp = lax.axis_size("dp")
    nx = X_CHIPS
    ny = seq // nx
    columns = [[y * nx + x for y in range(ny)] for x in range(nx)]

    def along_x(step):
        return [(y * nx + x, y * nx + (x + step) % nx) for y in range(ny) for x in range(nx)]

    right, left = along_x(1), along_x(-1)
    tokens = inputs_saved.shape[3]
    width = inputs_saved.shape[4]
    channels = grad_latent.shape[-1]
    piece = grad_latent.shape[3]

    both = lax.all_gather(grad_latent[0, 0][:, None], "seq", axis=1, tiled=True, axis_index_groups=columns)
    own = both
    far = nx // 2
    here = jnp.stack(
        [lax.rem(lax.axis_index("seq"), nx), lax.div(lax.axis_index("pipe"), pipe // 2)]
    )
    saved = jnp.swapaxes(inputs_saved[0, 0], 1, 2)
    vmem = pl.BlockSpec(memory_space=pltpu.VMEM)
    smem = pl.BlockSpec(memory_space=pltpu.SMEM)
    held = pltpu.VMEM((ny, nx, piece, channels), own.dtype)
    settings = pltpu.CompilerParams(vmem_limit_bytes=VMEM_BYTES)

    def kernel_call(body, out_shape, scratch, flops, here, *operands):
        return pl.pallas_call(
            body,
            out_shape=out_shape,
            in_specs=[smem] + [vmem] * len(operands),
            out_specs=(vmem,) * len(out_shape),
            scratch_shapes=scratch,
            compiler_params=settings,
            cost_estimate=pl.CostEstimate(
                flops=flops, bytes_accessed=4 * tokens * channels, transcendentals=0
            ),
        )(here, *operands)

    product = 2 * tokens * channels * width
    sums_shape = (jax.ShapeDtypeStruct((2, width, channels), jnp.float32),)
    from_left, from_right = [own], [own]
    for step in range(1, far):
        from_left.append(lax.ppermute(from_left[-1], "seq", right))
        from_right.append(lax.ppermute(from_right[-1], "seq", left))
    near = from_right[: far - 1] + from_left[1 : far - 1]
    picked_shape = jax.ShapeDtypeStruct((2, 3, ny, width, piece), saved.dtype)
    partial, picked = kernel_call(
        early_kernel, sums_shape + (picked_shape,), [held], 2 * product, here, *near, saved
    )
    from_left[-1], partial = lax.optimization_barrier((from_left[-1], partial))
    far_fwd = lax.ppermute(from_left[-1][0], "seq", right)
    far_rev = lax.ppermute(from_right[-1][1], "seq", left)
    third = (from_right[-1], from_left[-1])
    (total,) = kernel_call(
        third_kernel, sums_shape, [], product // 2, here, *third, partial, picked
    )
    share_shape = (dp, channels // dp, width)
    shares_fwd, grad = kernel_call(
        middle_kernel,
        (
            jax.ShapeDtypeStruct((1,) + share_shape, jnp.bfloat16),
            jax.ShapeDtypeStruct((width, tokens), own.dtype),
        ),
        [held],
        product,
        here,
        *near,
        *third,
        far_fwd,
        weights[0],
        total,
        picked,
    )
    (shares,) = kernel_call(
        late_kernel,
        (jax.ShapeDtypeStruct((2,) + share_shape, jnp.bfloat16),),
        [],
        product // 8,
        here,
        far_rev,
        total,
        picked,
        shares_fwd,
    )

    ends = [[p * dp + d for p in (i, pipe - 1 - i) for d in range(dp)] for i in range(pipe // 2)]
    shares = lax.all_to_all(
        shares.reshape(2 * dp, channels // dp, width),
        ("pipe", "dp"),
        0,
        0,
        tiled=True,
        axis_index_groups=ends,
    )
    weight_grad = jnp.sum(shares.astype(jnp.float32), axis=0) * (1.0 / tokens)
    return grad.T[None, None], weight_grad.T[None]


def solution(mesh):
    in_specs = (
        P("pipe", "dp", None, None, "seq"),
        P("pipe", "dp", None, "seq", None),
        P("pipe", "seq", None),
    )
    out_specs = (P("pipe", "dp", None, "seq"), P("pipe", "seq", "dp"))
    return jax.shard_map(local, mesh=mesh, in_specs=in_specs, out_specs=out_specs, check_vma=False)
```
